512 devices in a mesh: dp: 32 (over z, core), param: 16 (over y, x).
Axes of the slice: x: 4, y: 4, z: 16, core: 2. Of those that a mesh axis runs over, the one named last changes fastest.
Arguments:
- hidden: bfloat16 [64, 1024, 4096], P('dp', None, 'param'), may hold values from -6 to 6
- cotangent: bfloat16 [64, 1024, 4096], P('dp', None, 'param'), may hold values from -6 to 6
- adapter_down_weight: bfloat16 [4096, 8], P('param'), may hold values from -0.09375 to 0.09375
- adapter_up_weight: bfloat16 [8, 4096], P(None, 'param'), may hold values from -0.09375 to 0.09375
- lengths: int32 [64], P('dp'), may hold values from 128 to 1024, as said below
- precond: float32 [2, 32768], P(None, 'param'), may hold values from 0.2 to 5
- projection: bfloat16 [2, 32768, 8192], P(None, 'param', 'dp'), may hold values from -6 to 6
- targets: float32 [64, 8192], P(None, 'dp'), may hold values from -6 to 6
Outputs:
- scores: float32 [64, 64], P('param')
The draws below stay inside these ranges and needn't reach their ends.
Inputs may be any that keep to these rules, and one draw needn't show every extreme that they name: `lengths`: at least one sequence has all 1024 slots valid.
All inputs are finite; a program needn't handle non-finite values.
Results may differ from the reference program's by a relative error of at most 0.0041.
Values may be sent and summed in bfloat16 or wider, within the bound.
No kernel may reach another device: no remote copies, remote signals or barrier semaphores. Data moves between devices by JAX's collectives and lax.ppermute only.
A program may use at most 64 MiB of HBM per device.

```python
import math
import jax
import jax.numpy as jnp
from jax import lax

MODEL_WIDTH = 4096
ADAPTER_RANK = 8
K = 8192
NT = 64
LENGTH = 1024
SEQS = 64
PARAMS = 32768


def draw_lengths(key, part):
    key = jax.random.fold_in(key, 7)
    values = jax.random.randint(jax.random.fold_in(key, 1), (SEQS,), LENGTH // 8, LENGTH + 1)
    chosen = jax.random.randint(jax.random.fold_in(key, 2), (), 0, SEQS)
    return jnp.where(jnp.arange(SEQS) == chosen, LENGTH, values).astype(jnp.int32)


def steps_of(own_key, shape, split, least, high):
    factor_of = 1.0
    for position, shards_of in split:
        steps = jax.random.uniform(jax.random.fold_in(jax.random.fold_in(own_key, 6), position), (shards_of,), jnp.float32, least / len(split), high / len(split))
        factor_of = factor_of * jnp.repeat(jnp.exp(steps), shape[position] // shards_of).reshape((-1,) + (1,) * (len(shape) - 1 - position))
    return factor_of


def normal_values(stream_key, shape, spread, reach, shards=(), kind=jnp.bfloat16):
    factor_of = steps_of(stream_key, shape, shards, -0.22, 0.18) if shards else 1.0
    values = jax.random.normal(stream_key, shape, jnp.float32) * spread * factor_of
    return jnp.minimum(jnp.maximum(values, -reach), reach).astype(kind)


def setup_inputs(seed: int = 0) -> dict:
    seeds = jax.random.split(jax.random.key(seed), 9)
    hidden = normal_values(seeds[0], (SEQS, LENGTH, MODEL_WIDTH), 1.0, 6.0, ((0, 32), (2, 16)))
    cotangent = normal_values(seeds[1], (SEQS, LENGTH, MODEL_WIDTH), 1.0, 6.0, ((0, 32), (2, 16)))
    adapter_down_weight = normal_values(seeds[2], (MODEL_WIDTH, ADAPTER_RANK), MODEL_WIDTH ** -0.5, 0.09375, ((0, 16),))
    adapter_up_weight = normal_values(seeds[3], (ADAPTER_RANK, MODEL_WIDTH), MODEL_WIDTH ** -0.5, 0.09375, ((1, 16),))
    lengths = draw_lengths(jax.random.fold_in(seeds[8], 71), 0)
    precond = jnp.clip(jnp.exp(math.log(5.0) - 3.218876 * jax.random.uniform(seeds[5], (2, PARAMS), jnp.float32) ** steps_of(seeds[5], (2, PARAMS), ((1, 16),), -0.2, 0.2)), 0.2, 5.0)
    projection = normal_values(seeds[6], (2, PARAMS, K), 1.0, 6.0, ((1, 16), (2, 32)))
    targets = normal_values(seeds[7], (NT, K), 1.0, 6.0, ((1, 32),), jnp.float32)
    return {"hidden": hidden, "cotangent": cotangent, "adapter_down_weight": adapter_down_weight, "adapter_up_weight": adapter_up_weight, "lengths": lengths, "precond": precond, "projection": projection, "targets": targets}


def reference(hidden, cotangent, adapter_down_weight, adapter_up_weight, lengths, precond, projection, targets):

    def per_sequence(items):
        token_rows, output_gradient, valid_len = items
        lowrank_input = jnp.dot(token_rows, adapter_down_weight, preferred_element_type=jnp.float32)
        lowrank_backward = jnp.dot(output_gradient, adapter_up_weight.T, preferred_element_type=jnp.float32)
        valid = (jnp.arange(LENGTH, dtype=jnp.int32) < valid_len).astype(jnp.float32)[:, None]
        in_masked = (lowrank_input * valid).astype(jnp.bfloat16)
        back_masked = (lowrank_backward * valid).astype(jnp.bfloat16)
        grad_a = jnp.dot(token_rows.T, back_masked, preferred_element_type=jnp.float32)
        grad_b = jnp.dot(output_gradient.T, in_masked, preferred_element_type=jnp.float32)
        return jnp.stack([grad_a.reshape(-1), grad_b.reshape(-1)], axis=0)
    grads = lax.map(per_sequence, (hidden, cotangent, lengths))
    scaled = (grads * precond[None]).astype(jnp.bfloat16).reshape(SEQS, 2 * PARAMS)
    features = jnp.dot(scaled, projection.reshape(2 * PARAMS, K), preferred_element_type=jnp.float32)
    feat_sq = lax.optimization_barrier(jnp.sum(features * features, axis=1))
    target_sq = lax.optimization_barrier(jnp.sum(targets * targets, axis=1))
    products = jnp.dot(features, targets.T, precision=lax.Precision.HIGHEST)
    feat_scale = 1.0 / jnp.sqrt(feat_sq / K + 1e-06)
    target_scale = 1.0 / jnp.sqrt(target_sq / K + 1e-06)
    return products / math.sqrt(K) * feat_scale[:, None] * target_scale[None, :]
```

```python
import math

import jax
import jax.numpy as jnp
from jax import lax
from jax.sharding import PartitionSpec as P

K = 8192
f32 = jnp.float32
bf16 = jnp.bfloat16


def spread(block, axis, size, groups=None):
    copies = jnp.broadcast_to(block[None], (size,) + block.shape)
    return lax.all_to_all(copies, axis, 0, 0, axis_index_groups=groups)


def local(
    hidden, cotangent, adapter_down_weight, adapter_up_weight, lengths, precond, projection, targets
):
    seq_count, tok_count, _ = hidden.shape
    param = lax.axis_size("param")
    dp = lax.axis_size("dp")
    pairs = [[2 * z, 2 * z + 1] for z in range(dp // 2)]
    columns = [[2 * z + core for z in range(dp // 2)] for core in range(2)]

    low_in = jnp.einsum("mtx,xr->mrt", hidden, adapter_down_weight, preferred_element_type=f32)
    low_back = jnp.einsum("mtx,rx->mrt", cotangent, adapter_up_weight, preferred_element_type=f32)
    low = jnp.concatenate([low_in, low_back], axis=1).astype(bf16)
    low = jnp.sum(spread(low, "param", param).astype(f32), axis=0)
    valid = jnp.arange(tok_count, dtype=jnp.int32)[None, None, :] < lengths[:, None, None]
    masked = jnp.where(valid, low, 0.0).astype(bf16)
    rank = adapter_down_weight.shape[1]
    grad_a = jnp.einsum("etd,ert->edr", hidden, masked[:, rank:], preferred_element_type=f32)
    grad_b = jnp.einsum("etd,ert->edr", cotangent, masked[:, :rank], preferred_element_type=f32)
    stacked = jnp.stack([grad_a.reshape(seq_count, -1), grad_b.reshape(seq_count, -1)], axis=1)
    flat_grad = (stacked * precond[None]).astype(bf16).reshape(seq_count, -1)

    proj_rows = projection.reshape(-1, projection.shape[2])
    gathered = lax.all_gather(flat_grad, "dp", axis=0, tiled=True)
    partial_feats = jnp.dot(gathered, proj_rows, preferred_element_type=f32)

    shares = partial_feats.reshape(param, -1, partial_feats.shape[1])
    own_rows = jnp.sum(lax.all_to_all(shares, "param", 0, 0), axis=0)

    feat_sq = jnp.sum(own_rows * own_rows, axis=1)
    products = jnp.einsum("ek,tk->et", own_rows, targets, precision=lax.Precision.HIGHEST)
    target_sq = jnp.sum(targets * targets, axis=1)
    rows, count = products.shape
    stats = jnp.concatenate([products.reshape(-1), target_sq, feat_sq])
    stats = jnp.pad(stats, (0, -stats.shape[0] % 128)).reshape(-1, 128)
    stats = jnp.sum(lax.all_gather(stats, "dp", axis_index_groups=pairs), axis=0)
    stats = jnp.sum(spread(stats, "dp", dp // 2, columns), axis=0).reshape(-1)
    products = stats[: rows * count].reshape(rows, count)
    target_sq = stats[rows * count : (rows + 1) * count]
    feat_sq = stats[(rows + 1) * count : (rows + 1) * count + rows]
    feat_scale = 1.0 / jnp.sqrt(feat_sq / K + 1e-06)
    target_scale = 1.0 / jnp.sqrt(target_sq / K + 1e-06)
    return products / math.sqrt(K) * feat_scale[:, None] * target_scale[None, :]


def solution(mesh):
    return jax.shard_map(
        local,
        mesh=mesh,
        in_specs=(
            P("dp", None, "param"),
            P("dp", None, "param"),
            P("param", None),
            P(None, "param"),
            P("dp"),
            P(None, "param"),
            P(None, "param", "dp"),
            P(None, "dp"),
        ),
        out_specs=P("param", None),
        check_vma=False,
    )
```

```python
import math

import jax
import jax.numpy as jnp
from jax import lax
from jax.sharding import PartitionSpec as P

K = 8192
f32 = jnp.float32
bf16 = jnp.bfloat16


def spread(block, axis, size, groups=None):
    copies = jnp.broadcast_to(block[None], (size,) + block.shape)
    return lax.all_to_all(copies, axis, 0, 0, axis_index_groups=groups)


def local(
    hidden, cotangent, adapter_down_weight, adapter_up_weight, lengths, precond, projection, targets
):
    seq_count, tok_count, _ = hidden.shape
    param = lax.axis_size("param")
    dp = lax.axis_size("dp")
    columns = [[2 * z + core for z in range(dp // 2)] for core in range(2)]

    low_in = jnp.einsum("mtx,xr->mrt", hidden, adapter_down_weight, preferred_element_type=f32)
    low_back = jnp.einsum("mtx,rx->mrt", cotangent, adapter_up_weight, preferred_element_type=f32)
    low = jnp.concatenate([low_in, low_back], axis=1).astype(bf16)
    low = jnp.sum(spread(low, "param", param).astype(f32), axis=0)
    valid = jnp.arange(tok_count, dtype=jnp.int32)[None, None, :] < lengths[:, None, None]
    masked = jnp.where(valid, low, 0.0).astype(bf16)
    rank = adapter_down_weight.shape[1]
    grad_a = jnp.einsum("etd,ert->edr", hidden, masked[:, rank:], preferred_element_type=f32)
    grad_b = jnp.einsum("etd,ert->edr", cotangent, masked[:, :rank], preferred_element_type=f32)
    stacked = jnp.stack([grad_a.reshape(seq_count, -1), grad_b.reshape(seq_count, -1)], axis=1)
    flat_grad = (stacked * precond[None]).astype(bf16).reshape(seq_count, -1)

    proj_rows = projection.reshape(-1, projection.shape[2])
    mine = spread(flat_grad, "dp", dp // 2, columns)
    mine = mine.reshape(-1, flat_grad.shape[1])
    other = lax.ppermute(mine, "dp", [(i, i ^ 1) for i in range(dp)])
    feats = [jnp.dot(block, proj_rows, preferred_element_type=f32) for block in (mine, other)]
    feats = [block.reshape(param, -1, block.shape[1]) for block in feats]
    shares = jnp.concatenate(feats, axis=1)
    own_rows = jnp.sum(lax.all_to_all(shares, "param", 0, 0), axis=0)

    feat_sq = jnp.sum(own_rows * own_rows, axis=1)
    products = jnp.einsum("ek,tk->et", own_rows, targets, precision=lax.Precision.HIGHEST)
    target_sq = jnp.sum(targets * targets, axis=1)
    core = lax.axis_index("dp") % 2
    half = seq_count
    feat_sq = jnp.where(core == 0, feat_sq, jnp.roll(feat_sq, half, axis=0))
    products = jnp.where(core == 0, products, jnp.roll(products, half, axis=0))
    rows, count = products.shape
    stats = jnp.concatenate([products.reshape(-1), target_sq, feat_sq])
    stats = jnp.pad(stats, (0, -stats.shape[0] % 128)).reshape(-1, 128)
    stats = jnp.sum(spread(stats, "dp", dp), axis=0).reshape(-1)
    products = stats[: rows * count].reshape(rows, count)
    target_sq = stats[rows * count : (rows + 1) * count]
    feat_sq = stats[(rows + 1) * count : (rows + 1) * count + rows]
    feat_scale = 1.0 / jnp.sqrt(feat_sq / K + 1e-06)
    target_scale = 1.0 / jnp.sqrt(target_sq / K + 1e-06)
    return products / math.sqrt(K) * feat_scale[:, None] * target_scale[None, :]


def solution(mesh):
    return jax.shard_map(
        local,
        mesh=mesh,
        in_specs=(
            P("dp", None, "param"),
            P("dp", None, "param"),
            P("param", None),
            P(None, "param"),
            P("dp"),
            P(None, "param"),
            P(None, "param", "dp"),
            P(None, "dp"),
        ),
        out_specs=P("param", None),
        check_vma=False,
    )
```

```python
import math

import jax
import jax.numpy as jnp
from jax import lax
from jax.experimental import pallas as pl
from jax.experimental.pallas import tpu as pltpu
from jax.sharding import PartitionSpec as P

K = 8192
f32 = jnp.float32
bf16 = jnp.bfloat16
VMEM = pl.BlockSpec(memory_space=pltpu.VMEM)
HBM = pl.BlockSpec(memory_space=pltpu.HBM)
CHUNK = 1024


def cost(mib):
    return pl.CostEstimate(flops=0, bytes_accessed=mib * 2**22, transcendentals=0)


def low_kernel(hidden, cotangent, down, up, out, held_h, held_c, held_d, held_u, low, sem, out_sem):
    seqs, toks, _ = hidden.shape
    steps = toks // CHUNK
    weights = [
        pltpu.make_async_copy(src, dst, sem.at[which, seqs * steps])
        for which, (src, dst) in enumerate(((down, held_d), (up, held_u)))
    ]
    blocks = []
    for s in range(seqs):
        for t in range(steps):
            pair = []
            for which, (src, dst) in enumerate(((hidden, held_h), (cotangent, held_c))):
                part = (s, pl.ds(t * CHUNK, CHUNK))
                slot = sem.at[which, s * steps + t]
                pair.append(pltpu.make_async_copy(src.at[part], dst.at[part], slot))
            blocks.append(pair)
    for pair in [weights] + blocks:
        for copy in pair:
            copy.start()
    for copy in weights:
        copy.wait()
    contract = (((1,), (1,)), ((), ()))
    outs = []
    for s in range(seqs):
        for t in range(steps):
            halves = []
            span = pl.ds(t * CHUNK, CHUNK)
            pair = zip(blocks[s * steps + t], (held_d, held_u), (held_h, held_c))
            for copy, weight, held in pair:
                copy.wait()
                halves.append(
                    lax.dot_general(
                        weight[...], held[s, span, :], contract, preferred_element_type=f32
                    )
                )
            low[s, :, span] = jnp.concatenate(halves, axis=0).astype(bf16)
        for j in range(out.shape[0]):
            outs.append(pltpu.make_async_copy(low.at[s], out.at[j, s], out_sem.at[j, s]))
            outs[-1].start()
    for copy in outs:
        copy.wait()


def grad_kernel(lengths, parts, hidden, cotangent, precond, out):
    count, seqs, rows, toks = parts.shape
    rank = rows // 2
    for s in range(seqs):
        low = parts[0, s].astype(f32)
        for j in range(1, count):
            low = low + parts[j, s].astype(f32)
        valid = lax.broadcasted_iota(jnp.int32, (rows, toks), 1) < lengths[s]
        low = jnp.where(valid, low, 0.0)
        grads = []
        for half, data in ((low[rank:], hidden), (low[:rank], cotangent)):
            high = half.astype(bf16).astype(f32)
            both = jnp.concatenate([high, half - high], axis=0).astype(bf16)
            both = jnp.dot(both, data[s], preferred_element_type=f32)
            grads.append(both[:rank] + both[rank:])
        scaled = (jnp.concatenate(grads, axis=0) * precond[...]).astype(bf16)
        for z in range(out.shape[0]):
            out[z, s] = scaled


def feature_kernel(scaled, projection, other_projection, out):
    groups, seqs, _ = out.shape
    for core, block in enumerate((projection, other_projection)):
        feats = jnp.dot(scaled[...], block[...], preferred_element_type=f32)
        span = pl.ds(core * feats.shape[1], feats.shape[1])
        for j in range(groups):
            out[j, :, span] = feats[j * seqs : (j + 1) * seqs]


def local(
    hidden, cotangent, adapter_down_weight, adapter_up_weight, lengths, precond, projection, targets
):
    seqs, toks, width = hidden.shape
    rank = adapter_down_weight.shape[1]
    feats = projection.shape[2]
    param = lax.axis_size("param")
    dp = lax.axis_size("dp")
    columns = [[2 * z + core for z in range(dp // 2)] for core in range(2)]
    swap = [(i, i ^ 1) for i in range(dp)]
    params = pltpu.CompilerParams(vmem_limit_bytes=16 * 2**20)

    low = pl.pallas_call(
        low_kernel,
        out_shape=jax.ShapeDtypeStruct((param, seqs, 2 * rank, toks), bf16),
        in_specs=[HBM] * 4,
        out_specs=HBM,
        scratch_shapes=[
            pltpu.VMEM(hidden.shape, bf16),
            pltpu.VMEM(hidden.shape, bf16),
            pltpu.VMEM((rank, width), bf16),
            pltpu.VMEM((rank, width), bf16),
            pltpu.VMEM((seqs, 2 * rank, toks), bf16),
            pltpu.SemaphoreType.DMA((2, seqs * (toks // CHUNK) + 1)),
            pltpu.SemaphoreType.DMA((param, seqs)),
        ],
        cost_estimate=cost(1),
        name="low",
    )(hidden, cotangent, adapter_down_weight.T, adapter_up_weight)

    low, projection, targets = lax.optimization_barrier((low, projection, targets))
    parts = lax.all_to_all(low, "param", 0, 0)
    other_projection = lax.ppermute(projection, "dp", swap)
    other_targets = lax.ppermute(targets, "dp", swap)
    precond = precond.reshape(2, width, rank).transpose(0, 2, 1).reshape(2 * rank, width)

    scaled = pl.pallas_call(
        grad_kernel,
        out_shape=jax.ShapeDtypeStruct((dp // 2, seqs, 2 * rank, width), bf16),
        in_specs=[pl.BlockSpec(memory_space=pltpu.SMEM), VMEM, VMEM, VMEM, VMEM],
        out_specs=VMEM,
        compiler_params=params,
        cost_estimate=pl.CostEstimate(flops=10**12, bytes_accessed=2**22, transcendentals=0),
        name="grads",
    )(lengths, parts, hidden, cotangent, precond)
    scaled, projection, other_projection = lax.optimization_barrier(
        (scaled, projection, other_projection)
    )
    projection, other_projection = [
        block.reshape(2, width, rank, feats).transpose(0, 2, 1, 3).reshape(-1, feats)
        for block in (projection, other_projection)
    ]
    scaled = lax.all_to_all(scaled, "dp", 0, 0, axis_index_groups=columns)
    scaled = scaled.reshape(-1, 2 * rank * width)

    shares = pl.pallas_call(
        feature_kernel,
        out_shape=jax.ShapeDtypeStruct((param, seqs, 2 * feats), f32),
        in_specs=[VMEM] * 3,
        out_specs=VMEM,
        compiler_params=params,
        cost_estimate=cost(2),
        name="features",
    )(scaled, projection, other_projection)
    own_rows = jnp.sum(lax.all_to_all(shares, "param", 0, 0), axis=0)

    feat_sq = jnp.sum(own_rows * own_rows, axis=1)
    both_targets = jnp.concatenate([targets, other_targets], axis=1)
    products = jnp.einsum("ek,tk->et", own_rows, both_targets, precision=lax.Precision.HIGHEST)
    target_sq = jnp.sum(targets * targets, axis=1)
    count = products.shape[1]
    size = seqs * count
    stats = jnp.concatenate([products.reshape(-1), target_sq, feat_sq])
    stats = jnp.pad(stats, (0, -stats.shape[0] % 128)).reshape(-1, 128)
    stats = jnp.broadcast_to(stats[None], (dp,) + stats.shape)
    stats = lax.all_to_all(stats, "dp", 0, 0).reshape(dp // 2, 2, -1)
    stats = jnp.sum(stats, axis=0)
    products = stats[:, :size].reshape(2 * seqs, count)
    target_sq = stats[0, size : size + count] + stats[1, size : size + count]
    feat_sq = stats[:, size + count : size + count + seqs].reshape(-1)
    feat_scale = 1.0 / jnp.sqrt(feat_sq / K + 1e-06)
    target_scale = 1.0 / jnp.sqrt(target_sq / K + 1e-06)
    return products / math.sqrt(K) * feat_scale[:, None] * target_scale[None, :]


def solution(mesh):
    return jax.shard_map(
        local,
        mesh=mesh,
        in_specs=(
            P("dp", None, "param"),
            P("dp", None, "param"),
            P("param", None),
            P(None, "param"),
            P("dp"),
            P(None, "param"),
            P(None, "param", "dp"),
            P(None, "dp"),
        ),
        out_specs=P("param", None),
        check_vma=False,
    )
```

```python
import math

import jax
import jax.numpy as jnp
from jax import lax
from jax.experimental import pallas as pl
from jax.experimental.pallas import tpu as pltpu
from jax.sharding import PartitionSpec as P

K = 8192
f32 = jnp.float32
bf16 = jnp.bfloat16
VMEM = pl.BlockSpec(memory_space=pltpu.VMEM)
HBM = pl.BlockSpec(memory_space=pltpu.HBM)
CHUNK = 1024
SPLIT = 4


def cost(mib):
    return pl.CostEstimate(flops=0, bytes_accessed=mib * 2**22, transcendentals=0)


def low_kernel(hidden, cotangent, down, up, out, held_h, held_c, held_d, held_u, low, sem, out_sem):
    seqs, toks, _ = hidden.shape
    steps = toks // CHUNK
    weights = [
        pltpu.make_async_copy(src, dst, sem.at[which, seqs * steps])
        for which, (src, dst) in enumerate(((down, held_d), (up, held_u)))
    ]
    blocks = []
    for s in range(seqs):
        for t in range(steps):
            pair = []
            for which, (src, dst) in enumerate(((hidden, held_h), (cotangent, held_c))):
                part = (s, pl.ds(t * CHUNK, CHUNK))
                slot = sem.at[which, s * steps + t]
                pair.append(pltpu.make_async_copy(src.at[part], dst.at[part], slot))
            blocks.append(pair)
    for pair in [weights] + blocks:
        for copy in pair:
            copy.start()
    for copy in weights:
        copy.wait()
    contract = (((1,), (1,)), ((), ()))
    outs = []
    for s in range(seqs):
        for t in range(steps):
            halves = []
            span = pl.ds(t * CHUNK, CHUNK)
            pair = zip(blocks[s * steps + t], (held_d, held_u), (held_h, held_c))
            for copy, weight, held in pair:
                copy.wait()
                halves.append(
                    lax.dot_general(
                        weight[...], held[s, span, :], contract, preferred_element_type=f32
                    )
                )
            low[s, :, span] = jnp.concatenate(halves, axis=0).astype(bf16)
        for j in range(out.shape[0]):
            outs.append(pltpu.make_async_copy(low.at[s], out.at[j, s], out_sem.at[j, s]))
            outs[-1].start()
    for copy in outs:
        copy.wait()


def grad_kernel(lengths, parts, hidden, cotangent, precond, out):
    count, seqs, rows, toks = parts.shape
    rank = rows // 2
    for s in range(seqs):
        low = parts[0, s].astype(f32)
        for j in range(1, count):
            low = low + parts[j, s].astype(f32)
        valid = lax.broadcasted_iota(jnp.int32, (rows, toks), 1) < lengths[s]
        low = jnp.where(valid, low, 0.0)
        grads = []
        for half, data in ((low[rank:], hidden), (low[:rank], cotangent)):
            high = half.astype(bf16).astype(f32)
            both = jnp.concatenate([high, half - high], axis=0).astype(bf16)
            both = jnp.dot(both, data[s], preferred_element_type=f32)
            grads.append(both[:rank] + both[rank:])
        scaled = (jnp.concatenate(grads, axis=0) * precond[...]).astype(bf16)
        for z in range(out.shape[0]):
            out[z, s] = scaled


def feature_kernel(scaled, projection, other_projection, out, held, sem):
    groups, seqs, _ = out.shape
    rows = held.shape[0] // SPLIT
    parts = [pl.ds(i * rows, rows) for i in range(SPLIT)]
    copies = [
        pltpu.make_async_copy(other_projection.at[part], held.at[part], sem.at[i])
        for i, part in enumerate(parts)
    ]
    for copy in copies:
        copy.start()

    def put(feats, core):
        span = pl.ds(core * feats.shape[1], feats.shape[1])
        for j in range(groups):
            out[j, :, span] = feats[j * seqs : (j + 1) * seqs]

    put(jnp.dot(scaled[...], projection[...], preferred_element_type=f32), 0)
    total = None
    for copy, part in zip(copies, parts):
        copy.wait()
        term = jnp.dot(scaled[:, part], held[part, :], preferred_element_type=f32)
        total = term if total is None else total + term
    put(total, 1)


def local(
    hidden, cotangent, adapter_down_weight, adapter_up_weight, lengths, precond, projection, targets
):
    seqs, toks, width = hidden.shape
    rank = adapter_down_weight.shape[1]
    feats = projection.shape[2]
    param = lax.axis_size("param")
    dp = lax.axis_size("dp")
    columns = [[2 * z + core for z in range(dp // 2)] for core in range(2)]
    swap = [(i, i ^ 1) for i in range(dp)]
    params = pltpu.CompilerParams(vmem_limit_bytes=16 * 2**20)

    low = pl.pallas_call(
        low_kernel,
        out_shape=jax.ShapeDtypeStruct((param, seqs, 2 * rank, toks), bf16),
        in_specs=[HBM] * 4,
        out_specs=HBM,
        scratch_shapes=[
            pltpu.VMEM(hidden.shape, bf16),
            pltpu.VMEM(hidden.shape, bf16),
            pltpu.VMEM((rank, width), bf16),
            pltpu.VMEM((rank, width), bf16),
            pltpu.VMEM((seqs, 2 * rank, toks), bf16),
            pltpu.SemaphoreType.DMA((2, seqs * (toks // CHUNK) + 1)),
            pltpu.SemaphoreType.DMA((param, seqs)),
        ],
        cost_estimate=cost(1),
        name="low",
    )(hidden, cotangent, adapter_down_weight.T, adapter_up_weight)

    low, projection, targets = lax.optimization_barrier((low, projection, targets))
    parts = lax.all_to_all(low, "param", 0, 0)
    other_projection = lax.ppermute(projection, "dp", swap)
    other_targets = lax.ppermute(targets, "dp", swap)
    precond = precond.reshape(2, width, rank).transpose(0, 2, 1).reshape(2 * rank, width)

    scaled = pl.pallas_call(
        grad_kernel,
        out_shape=jax.ShapeDtypeStruct((dp // 2, seqs, 2 * rank, width), bf16),
        in_specs=[pl.BlockSpec(memory_space=pltpu.SMEM), VMEM, VMEM, VMEM, VMEM],
        out_specs=VMEM,
        compiler_params=params,
        cost_estimate=pl.CostEstimate(flops=10**12, bytes_accessed=2**22, transcendentals=0),
        name="grads",
    )(lengths, parts, hidden, cotangent, precond)
    scaled, projection, other_projection = lax.optimization_barrier(
        (scaled, projection, other_projection)
    )
    projection, other_projection = [
        block.reshape(2, width, rank, feats).transpose(0, 2, 1, 3).reshape(-1, feats)
        for block in (projection, other_projection)
    ]
    scaled = lax.all_to_all(scaled, "dp", 0, 0, axis_index_groups=columns)
    target_sq = jnp.sum(targets * targets, axis=1)
    both_targets = jnp.concatenate([targets, other_targets], axis=1)
    scaled, target_sq, both_targets = lax.optimization_barrier((scaled, target_sq, both_targets))
    scaled = scaled.reshape(-1, 2 * rank * width)

    shares = pl.pallas_call(
        feature_kernel,
        out_shape=jax.ShapeDtypeStruct((param, seqs, 2 * feats), f32),
        in_specs=[VMEM, VMEM, HBM],
        out_specs=VMEM,
        scratch_shapes=[
            pltpu.VMEM((2 * rank * width, feats), bf16),
            pltpu.SemaphoreType.DMA((SPLIT,)),
        ],
        compiler_params=pltpu.CompilerParams(vmem_limit_bytes=51 * 2**20),
        cost_estimate=cost(2),
        name="features",
    )(scaled, projection, other_projection)
    own_rows = jnp.sum(lax.all_to_all(shares, "param", 0, 0), axis=0)

    feat_sq = jnp.sum(own_rows * own_rows, axis=1)
    products = jnp.einsum("ek,tk->et", own_rows, both_targets, precision=lax.Precision.HIGHEST)
    count = products.shape[1]
    size = seqs * count
    stats = jnp.concatenate([products.reshape(-1), target_sq, feat_sq])
    stats = jnp.pad(stats, (0, -stats.shape[0] % 128)).reshape(-1, 128)
    stats = jnp.broadcast_to(stats[None], (dp,) + stats.shape)
    stats = lax.all_to_all(stats, "dp", 0, 0).reshape(dp // 2, 2, -1)
    stats = jnp.sum(stats, axis=0)
    products = stats[:, :size].reshape(2 * seqs, count)
    target_sq = stats[0, size : size + count] + stats[1, size : size + count]
    feat_sq = stats[:, size + count : size + count + seqs].reshape(-1)
    feat_scale = 1.0 / jnp.sqrt(feat_sq / K + 1e-06)
    target_scale = 1.0 / jnp.sqrt(target_sq / K + 1e-06)
    return products / math.sqrt(K) * feat_scale[:, None] * target_scale[None, :]


def solution(mesh):
    return jax.shard_map(
        local,
        mesh=mesh,
        in_specs=(
            P("dp", None, "param"),
            P("dp", None, "param"),
            P("param", None),
            P(None, "param"),
            P("dp"),
            P(None, "param"),
            P(None, "param", "dp"),
            P(None, "dp"),
        ),
        out_specs=P("param", None),
        check_vma=False,
    )
```

```python
import math

import jax
import jax.numpy as jnp
from jax import lax
from jax.experimental import pallas as pl
from jax.experimental.pallas import tpu as pltpu
from jax.sharding import PartitionSpec as P

K = 8192
f32 = jnp.float32
bf16 = jnp.bfloat16
VMEM = pl.BlockSpec(memory_space=pltpu.VMEM)
HBM = pl.BlockSpec(memory_space=pltpu.HBM)
CHUNK = 1024
SPLIT = 4


def cost(mib):
    return pl.CostEstimate(flops=0, bytes_accessed=mib * 2**22, transcendentals=0)


def low_kernel(hidden, cotangent, down, up, out, held_h, held_c, held_d, held_u, low, sem, out_sem):
    seqs, toks, _ = hidden.shape
    steps = toks // CHUNK
    weights = [
        pltpu.make_async_copy(src, dst, sem.at[which, seqs * steps])
        for which, (src, dst) in enumerate(((down, held_d), (up, held_u)))
    ]
    blocks = []
    for s in range(seqs):
        for t in range(steps):
            pair = []
            for which, (src, dst) in enumerate(((hidden, held_h), (cotangent, held_c))):
                part = (s, pl.ds(t * CHUNK, CHUNK))
                slot = sem.at[which, s * steps + t]
                pair.append(pltpu.make_async_copy(src.at[part], dst.at[part], slot))
            blocks.append(pair)
    for pair in [weights] + blocks:
        for copy in pair:
            copy.start()
    for copy in weights:
        copy.wait()
    contract = (((1,), (1,)), ((), ()))
    outs = []
    for s in range(seqs):
        for t in range(steps):
            halves = []
            span = pl.ds(t * CHUNK, CHUNK)
            pair = zip(blocks[s * steps + t], (held_d, held_u), (held_h, held_c))
            for copy, weight, held in pair:
                copy.wait()
                halves.append(
                    lax.dot_general(
                        weight[...], held[s, span, :], contract, preferred_element_type=f32
                    )
                )
            low[s, :, span] = jnp.concatenate(halves, axis=0).astype(bf16)
        for j in range(out.shape[0]):
            outs.append(pltpu.make_async_copy(low.at[s], out.at[j, s], out_sem.at[j, s]))
            outs[-1].start()
    for copy in outs:
        copy.wait()


def grad_kernel(lengths, parts, hidden, cotangent, precond, out):
    count, seqs, rows, toks = parts.shape
    rank = rows // 2
    for s in range(seqs):
        low = parts[0, s].astype(f32)
        for j in range(1, count):
            low = low + parts[j, s].astype(f32)
        valid = lax.broadcasted_iota(jnp.int32, (rows, toks), 1) < lengths[s]
        low = jnp.where(valid, low, 0.0)
        grads = []
        for half, data in ((low[rank:], hidden), (low[:rank], cotangent)):
            high = half.astype(bf16).astype(f32)
            both = jnp.concatenate([high, half - high], axis=0).astype(bf16)
            both = jnp.dot(both, data[s], preferred_element_type=f32)
            grads.append(both[:rank] + both[rank:])
        scaled = (jnp.concatenate(grads, axis=0) * precond[...]).astype(bf16)
        for z in range(out.shape[0]):
            out[z, s] = scaled


def feature_kernel(scaled, projection, other_projection, out, held, sem):
    groups, seqs, _ = out.shape
    rows = held.shape[0] // SPLIT
    parts = [pl.ds(i * rows, rows) for i in range(SPLIT)]
    copies = [
        pltpu.make_async_copy(other_projection.at[part], held.at[part], sem.at[i])
        for i, part in enumerate(parts)
    ]
    for copy in copies:
        copy.start()

    def put(feats, core):
        span = pl.ds(core * feats.shape[1], feats.shape[1])
        for j in range(groups):
            out[j, :, span] = feats[j * seqs : (j + 1) * seqs]

    put(jnp.dot(scaled[...], projection[...], preferred_element_type=f32), 0)
    total = None
    for copy, part in zip(copies, parts):
        copy.wait()
        term = jnp.dot(scaled[:, part], held[part, :], preferred_element_type=f32)
        total = term if total is None else total + term
    put(total, 1)


def stats_kernel(shares, targets, other_targets, out):
    own = jnp.sum(shares[...], axis=0)
    feats = targets.shape[1]
    contract = (((1,), (1,)), ((), ()))
    rows, count = own.shape[0], targets.shape[0]

    def times(left, right):
        return lax.dot_general(
            left, right, contract, precision=lax.Precision.HIGHEST, preferred_element_type=f32
        )

    products = times(own[:, :feats], targets[...]) + times(own[:, feats:], other_targets[...])
    squares = jnp.sum(own * own, axis=1, keepdims=True)
    squares = [jnp.broadcast_to(squares[i : i + 1], (1, count // rows)) for i in range(rows)]
    target_sq = times(jnp.ones((8, feats), f32), targets[...] * targets[...])[:1]
    first = jnp.concatenate([products[:1], target_sq], axis=1)
    last = jnp.concatenate([products[1:]] + squares, axis=1)
    both = jnp.concatenate([first, last], axis=0)
    for d in range(out.shape[0]):
        out[d] = both


def score_kernel(stats, out):
    total = jnp.sum(stats[...], axis=0)
    count = out.shape[1]
    rows = total.shape[1]
    target_sq = total[0, :1, count:] + total[1, :1, count:]
    target_scale = 1.0 / jnp.sqrt(target_sq / K + 1e-06)
    for core in range(2):
        for i in range(rows):
            at = count + i * (count // rows)
            feat_scale = 1.0 / jnp.sqrt(total[core, 1:, at : at + 1] / K + 1e-06)
            scores = total[core, i : i + 1, :count] / math.sqrt(K) * feat_scale * target_scale
            out[core * rows + i : core * rows + i + 1] = scores


def local(
    hidden, cotangent, adapter_down_weight, adapter_up_weight, lengths, precond, projection, targets
):
    seqs, toks, width = hidden.shape
    rank = adapter_down_weight.shape[1]
    feats = projection.shape[2]
    param = lax.axis_size("param")
    dp = lax.axis_size("dp")
    columns = [[2 * z + core for z in range(dp // 2)] for core in range(2)]
    swap = [(i, i ^ 1) for i in range(dp)]
    params = pltpu.CompilerParams(vmem_limit_bytes=16 * 2**20)

    low = pl.pallas_call(
        low_kernel,
        out_shape=jax.ShapeDtypeStruct((param, seqs, 2 * rank, toks), bf16),
        in_specs=[HBM] * 4,
        out_specs=HBM,
        scratch_shapes=[
            pltpu.VMEM(hidden.shape, bf16),
            pltpu.VMEM(hidden.shape, bf16),
            pltpu.VMEM((rank, width), bf16),
            pltpu.VMEM((rank, width), bf16),
            pltpu.VMEM((seqs, 2 * rank, toks), bf16),
            pltpu.SemaphoreType.DMA((2, seqs * (toks // CHUNK) + 1)),
            pltpu.SemaphoreType.DMA((param, seqs)),
        ],
        cost_estimate=cost(1),
        name="low",
    )(hidden, cotangent, adapter_down_weight.T, adapter_up_weight)

    low, projection, targets = lax.optimization_barrier((low, projection, targets))
    parts = lax.all_to_all(low, "param", 0, 0)
    other_projection = lax.ppermute(projection, "dp", swap)
    other_targets = lax.ppermute(targets, "dp", swap)
    precond = precond.reshape(2, width, rank).transpose(0, 2, 1).reshape(2 * rank, width)

    scaled = pl.pallas_call(
        grad_kernel,
        out_shape=jax.ShapeDtypeStruct((dp // 2, seqs, 2 * rank, width), bf16),
        in_specs=[pl.BlockSpec(memory_space=pltpu.SMEM), VMEM, VMEM, VMEM, VMEM],
        out_specs=VMEM,
        compiler_params=params,
        cost_estimate=pl.CostEstimate(flops=10**12, bytes_accessed=2**22, transcendentals=0),
        name="grads",
    )(lengths, parts, hidden, cotangent, precond)
    scaled, projection, other_projection = lax.optimization_barrier(
        (scaled, projection, other_projection)
    )
    projection, other_projection = [
        block.reshape(2, width, rank, feats).transpose(0, 2, 1, 3).reshape(-1, feats)
        for block in (projection, other_projection)
    ]
    scaled = lax.all_to_all(scaled, "dp", 0, 0, axis_index_groups=columns)
    scaled, other_targets = lax.optimization_barrier((scaled, other_targets))
    scaled = scaled.reshape(-1, 2 * rank * width)

    shares = pl.pallas_call(
        feature_kernel,
        out_shape=jax.ShapeDtypeStruct((param, seqs, 2 * feats), f32),
        in_specs=[VMEM, VMEM, HBM],
        out_specs=VMEM,
        scratch_shapes=[
            pltpu.VMEM((2 * rank * width, feats), bf16),
            pltpu.SemaphoreType.DMA((SPLIT,)),
        ],
        compiler_params=pltpu.CompilerParams(vmem_limit_bytes=51 * 2**20),
        cost_estimate=cost(2),
        name="features",
    )(scaled, projection, other_projection)
    shares = lax.all_to_all(shares, "param", 0, 0)
    count = targets.shape[0]
    stats = pl.pallas_call(
        stats_kernel,
        out_shape=jax.ShapeDtypeStruct((dp, seqs, 2 * count), f32),
        in_specs=[VMEM] * 3,
        out_specs=VMEM,
        compiler_params=params,
        name="stats",
    )(shares, targets, other_targets)
    stats = lax.all_to_all(stats, "dp", 0, 0).reshape(dp // 2, 2, seqs, 2 * count)
    return pl.pallas_call(
        score_kernel,
        out_shape=jax.ShapeDtypeStruct((2 * seqs, count), f32),
        in_specs=[VMEM],
        out_specs=VMEM,
        compiler_params=params,
        name="scores",
    )(stats)


def solution(mesh):
    return jax.shard_map(
        local,
        mesh=mesh,
        in_specs=(
            P("dp", None, "param"),
            P("dp", None, "param"),
            P("param", None),
            P(None, "param"),
            P("dp"),
            P(None, "param"),
            P(None, "param", "dp"),
            P(None, "dp"),
        ),
        out_specs=P("param", None),
        check_vma=False,
    )
```

```python
import math

import jax
import jax.numpy as jnp
from jax import lax
from jax.experimental import pallas as pl
from jax.experimental.pallas import tpu as pltpu
from jax.sharding import PartitionSpec as P

K = 8192
f32 = jnp.float32
bf16 = jnp.bfloat16
VMEM = pl.BlockSpec(memory_space=pltpu.VMEM)
HBM = pl.BlockSpec(memory_space=pltpu.HBM)
CHUNK = 1024


def cost(mib):
    return pl.CostEstimate(flops=0, bytes_accessed=mib * 2**22, transcendentals=0)


def low_kernel(hidden, cotangent, down, up, out, held_h, held_c, held_d, held_u, low, sem, out_sem):
    seqs, toks, _ = hidden.shape
    steps = toks // CHUNK
    weights = [
        pltpu.make_async_copy(src, dst, sem.at[which, seqs * steps])
        for which, (src, dst) in enumerate(((down, held_d), (up, held_u)))
    ]
    blocks = []
    for s in range(seqs):
        for t in range(steps):
            pair = []
            for which, (src, dst) in enumerate(((hidden, held_h), (cotangent, held_c))):
                part = (s, pl.ds(t * CHUNK, CHUNK))
                slot = sem.at[which, s * steps + t]
                pair.append(pltpu.make_async_copy(src.at[part], dst.at[part], slot))
            blocks.append(pair)
    for pair in [weights] + blocks:
        for copy in pair:
            copy.start()
    for copy in weights:
        copy.wait()
    contract = (((1,), (1,)), ((), ()))
    outs = []
    for s in range(seqs):
        for t in range(steps):
            halves = []
            span = pl.ds(t * CHUNK, CHUNK)
            pair = zip(blocks[s * steps + t], (held_d, held_u), (held_h, held_c))
            for copy, weight, held in pair:
                copy.wait()
                halves.append(
                    lax.dot_general(
                        weight[...], held[s, span, :], contract, preferred_element_type=f32
                    )
                )
            low[s, :, span] = jnp.concatenate(halves, axis=0).astype(bf16)
        for j in range(out.shape[0]):
            outs.append(pltpu.make_async_copy(low.at[s], out.at[j, s], out_sem.at[j, s]))
            outs[-1].start()
    for copy in outs:
        copy.wait()


def grad_kernel(lengths, parts, hidden, cotangent, precond, out):
    count, seqs, rows, toks = parts.shape
    rank = rows // 2
    for s in range(seqs):
        low = parts[0, s].astype(f32)
        for j in range(1, count):
            low = low + parts[j, s].astype(f32)
        valid = lax.broadcasted_iota(jnp.int32, (rows, toks), 1) < lengths[s]
        low = jnp.where(valid, low, 0.0)
        grads = []
        for half, data in ((low[rank:], hidden), (low[:rank], cotangent)):
            high = half.astype(bf16).astype(f32)
            both = jnp.concatenate([high, half - high], axis=0).astype(bf16)
            both = jnp.dot(both, data[s], preferred_element_type=f32)
            grads.append(both[:rank] + both[rank:])
        scaled = (jnp.concatenate(grads, axis=0) * precond[...]).astype(bf16)
        for z in range(out.shape[0]):
            out[z, s] = scaled


def feature_kernel(scaled, own_a, own_b, other_a, other_b, out):
    groups, seqs, _ = out.shape
    half = own_a.shape[0]
    for core, (first, last) in enumerate(((own_a, own_b), (other_a, other_b))):
        feats = jnp.dot(scaled[:, :half], first[...], preferred_element_type=f32)
        feats = feats + jnp.dot(scaled[:, half:], last[...], preferred_element_type=f32)
        span = pl.ds(core * feats.shape[1], feats.shape[1])
        for j in range(groups):
            out[j, :, span] = feats[j * seqs : (j + 1) * seqs]


def stats_kernel(shares, targets, other_targets, out):
    own = jnp.sum(shares[...], axis=0)
    feats = targets.shape[1]
    contract = (((1,), (1,)), ((), ()))
    rows, count = own.shape[0], targets.shape[0]

    def times(left, right):
        return lax.dot_general(
            left, right, contract, precision=lax.Precision.HIGHEST, preferred_element_type=f32
        )

    products = times(own[:, :feats], targets[...]) + times(own[:, feats:], other_targets[...])
    squares = jnp.sum(own * own, axis=1, keepdims=True)
    squares = [jnp.broadcast_to(squares[i : i + 1], (1, count // rows)) for i in range(rows)]
    target_sq = times(jnp.ones((8, feats), f32), targets[...] * targets[...])[:1]
    first = jnp.concatenate([products[:1], target_sq], axis=1)
    last = jnp.concatenate([products[1:]] + squares, axis=1)
    both = jnp.concatenate([first, last], axis=0)
    for d in range(out.shape[0]):
        out[d] = both


def score_kernel(stats, out):
    total = jnp.sum(stats[...], axis=0)
    count = out.shape[1]
    rows = total.shape[1]
    target_sq = total[0, :1, count:] + total[1, :1, count:]
    target_scale = 1.0 / jnp.sqrt(target_sq / K + 1e-06)
    for core in range(2):
        for i in range(rows):
            at = count + i * (count // rows)
            feat_scale = 1.0 / jnp.sqrt(total[core, 1:, at : at + 1] / K + 1e-06)
            scores = total[core, i : i + 1, :count] / math.sqrt(K) * feat_scale * target_scale
            out[core * rows + i : core * rows + i + 1] = scores


def local(
    hidden, cotangent, adapter_down_weight, adapter_up_weight, lengths, precond, projection, targets
):
    seqs, toks, width = hidden.shape
    rank = adapter_down_weight.shape[1]
    feats = projection.shape[2]
    param = lax.axis_size("param")
    dp = lax.axis_size("dp")
    columns = [[2 * z + core for z in range(dp // 2)] for core in range(2)]
    swap = [(i, i ^ 1) for i in range(dp)]
    params = pltpu.CompilerParams(vmem_limit_bytes=16 * 2**20)

    low = pl.pallas_call(
        low_kernel,
        out_shape=jax.ShapeDtypeStruct((param, seqs, 2 * rank, toks), bf16),
        in_specs=[HBM] * 4,
        out_specs=HBM,
        scratch_shapes=[
            pltpu.VMEM(hidden.shape, bf16),
            pltpu.VMEM(hidden.shape, bf16),
            pltpu.VMEM((rank, width), bf16),
            pltpu.VMEM((rank, width), bf16),
            pltpu.VMEM((seqs, 2 * rank, toks), bf16),
            pltpu.SemaphoreType.DMA((2, seqs * (toks // CHUNK) + 1)),
            pltpu.SemaphoreType.DMA((param, seqs)),
        ],
        cost_estimate=cost(1),
        name="low",
    )(hidden, cotangent, adapter_down_weight.T, adapter_up_weight)

    low, projection, targets = lax.optimization_barrier((low, projection, targets))
    parts = lax.all_to_all(low, "param", 0, 0)
    other_projection = lax.ppermute(projection, "dp", swap)
    other_targets = lax.ppermute(targets, "dp", swap)
    precond = precond.reshape(2, width, rank).transpose(0, 2, 1).reshape(2 * rank, width)

    scaled = pl.pallas_call(
        grad_kernel,
        out_shape=jax.ShapeDtypeStruct((dp // 2, seqs, 2 * rank, width), bf16),
        in_specs=[pl.BlockSpec(memory_space=pltpu.SMEM), VMEM, VMEM, VMEM, VMEM],
        out_specs=VMEM,
        compiler_params=params,
        cost_estimate=pl.CostEstimate(flops=10**12, bytes_accessed=2**22, transcendentals=0),
        name="grads",
    )(lengths, parts, hidden, cotangent, precond)
    scaled, projection, other_projection = lax.optimization_barrier(
        (scaled, projection, other_projection)
    )
    blocks = [
        half.reshape(width, rank, feats).transpose(1, 0, 2).reshape(-1, feats)
        for block in (projection, other_projection)
        for half in block
    ]
    scaled = lax.all_to_all(scaled, "dp", 0, 0, axis_index_groups=columns)
    scaled, other_targets = lax.optimization_barrier((scaled, other_targets))
    scaled = scaled.reshape(-1, 2 * rank * width)

    shares = pl.pallas_call(
        feature_kernel,
        out_shape=jax.ShapeDtypeStruct((param, seqs, 2 * feats), f32),
        in_specs=[VMEM] * 5,
        out_specs=VMEM,
        compiler_params=params,
        cost_estimate=cost(2),
        name="features",
    )(scaled, *blocks)
    shares = lax.all_to_all(shares, "param", 0, 0)
    count = targets.shape[0]
    stats = pl.pallas_call(
        stats_kernel,
        out_shape=jax.ShapeDtypeStruct((dp, seqs, 2 * count), f32),
        in_specs=[VMEM] * 3,
        out_specs=VMEM,
        compiler_params=params,
        name="stats",
    )(shares, targets, other_targets)
    stats = lax.all_to_all(stats, "dp", 0, 0).reshape(dp // 2, 2, seqs, 2 * count)
    return pl.pallas_call(
        score_kernel,
        out_shape=jax.ShapeDtypeStruct((2 * seqs, count), f32),
        in_specs=[VMEM],
        out_specs=VMEM,
        compiler_params=params,
        name="scores",
    )(stats)


def solution(mesh):
    return jax.shard_map(
        local,
        mesh=mesh,
        in_specs=(
            P("dp", None, "param"),
            P("dp", None, "param"),
            P("param", None),
            P(None, "param"),
            P("dp"),
            P(None, "param"),
            P(None, "param", "dp"),
            P(None, "dp"),
        ),
        out_specs=P("param", None),
        check_vma=False,
    )
```
